32 devices in a mesh: seq: 8 (over y, x, core), chan: 4 (over z).
Axes of the slice: x: 2, y: 2, z: 4, core: 2. Of those that a mesh axis runs over, the one named last changes fastest.
Arguments:
- layer_input: bfloat16 [1024, 4096], P('seq', 'chan'), may hold values from -6 to 6
- gate_query: bfloat16 [1024, 4096], P('seq', 'chan'), may hold values from -6 to 6
- gate_key: bfloat16 [1024, 4096], P('seq', 'chan'), may hold values from -6 to 6
- value_proj: bfloat16 [1024, 4096], P('seq', 'chan'), may hold values from -6 to 6
- grad_out: bfloat16 [1024, 4096], P('seq', 'chan'), may hold values from -6 to 6
- filter_taps: bfloat16 [1024, 4096], P('seq', 'chan'), may hold values from -1.1 to 1.1
Outputs:
- grad_query: bfloat16 [1024, 4096], P('seq', 'chan')
- grad_key: bfloat16 [1024, 4096], P('seq', 'chan')
- grad_value: bfloat16 [1024, 4096], P('seq', 'chan')
- grad_filter: bfloat16 [1024, 4096], P('seq', 'chan')
- grad_weight: float32 [4096, 4096], P('seq', 'chan')
The draws below stay inside these ranges and needn't reach their ends.
All inputs are finite; a program needn't handle non-finite values.
Results may differ from the reference program's by a relative error of at most 0.0067.
Values may be sent and summed in bfloat16 or wider, within the bound.
A program may use at most 128 MiB of HBM per device.

```python
import math
import jax
import jax.numpy as jnp
from jax import lax

D = 4096
P_SIZE = 128
LENGTH = 1024


def draw_filter_taps(key, part):
    first, second = jax.random.split(jax.random.fold_in(key, 17))
    rates = jax.random.uniform(first, (1, D), minval=math.log(30.0), maxval=math.log(4.0 * LENGTH))
    noise = jnp.clip(jax.random.normal(second, (LENGTH, D)), -4.0, 4.0)
    spans = jnp.exp(rates)
    places = jnp.arange(LENGTH, dtype=jnp.float32)[:, None]
    kept = jnp.minimum(spans, float(LENGTH))
    taps = noise * jnp.exp(-places / spans) * jnp.sqrt(2.0 / kept)
    return taps.astype(jnp.float32).astype(jnp.bfloat16)


def strengthened(values, stream_key, source, target, shards_of, factor):
    def block_of(position):
        return (jnp.arange(values.shape[position]) // (values.shape[position] // shards_of)).reshape((-1,) + (1,) * (values.ndim - 1 - position))

    near = jax.random.permutation(stream_key, shards_of)[block_of(target)]
    far = (block_of(target) + shards_of // 2) % shards_of
    return jnp.where((block_of(source) == near) | (block_of(source) == far), factor * values, values)


def shard_levels(stream_key, extent, cuts, smallest, largest):
    gain, own = 1.0, jax.random.fold_in(stream_key, 6)
    for position, shards_of in cuts:
        steps = jnp.exp(jax.random.uniform(jax.random.fold_in(own, position), (shards_of,), jnp.float32, smallest / len(cuts), largest / len(cuts)))
        gain = gain * jnp.repeat(steps, extent[position] // shards_of).reshape([-1 if axis == position else 1 for axis in range(len(extent))])
    return gain


def gaussian(rng, dims, scale, most, cuts=(), kind=jnp.bfloat16):
    drawn = scale * jax.random.normal(rng, dims, jnp.float32)
    if cuts:
        drawn = drawn * shard_levels(rng, dims, cuts, -0.22, 0.18)
    return jnp.clip(drawn, -most, most).astype(kind)


def gaussian_with(own_key, extent, scale, limit, cuts, heavy, kind=jnp.bfloat16):
    values = scale * jax.random.normal(own_key, extent, jnp.float32)
    if cuts:
        values = values * shard_levels(own_key, extent, cuts, -0.22, 0.18)
    return jnp.clip(strengthened(values, jax.random.fold_in(own_key, 3), *heavy), -limit, limit).astype(kind)


def setup_inputs(seed: int = 0) -> dict:
    streams_of = jax.random.split(jax.random.key(seed), 7)
    return {
        "layer_input": gaussian_with(streams_of[0], (LENGTH, D), 1.0, 6.0, ((0, 8), (1, 4)), (0, 1, 8, 2.0)),
        "gate_query": gaussian(streams_of[1], (LENGTH, D), 1.0, 6.0, ((0, 8), (1, 4))),
        "gate_key": gaussian(streams_of[2], (LENGTH, D), 1.0, 6.0, ((0, 8), (1, 4))),
        "value_proj": gaussian(streams_of[3], (LENGTH, D), 1.0, 6.0, ((0, 8), (1, 4))),
        "grad_out": gaussian(streams_of[4], (LENGTH, D), 1.0, 6.0, ((0, 8), (1, 4))),
        "filter_taps": draw_filter_taps(jax.random.fold_in(streams_of[6], 71), 0),
    }


def angle_grid(first, second, period):
    product = first[:, None] * second[None, :] % period
    return product.astype(jnp.float32) * (2.0 * math.pi / period)

def round_back(array):
    return lax.optimization_barrier(array.astype(jnp.bfloat16)).astype(jnp.float32)

def transform(signal):
    blocks = LENGTH // P_SIZE
    width = signal.shape[1]
    shaped = signal.astype(jnp.float32).reshape(blocks, P_SIZE, width)
    padded = jnp.concatenate([shaped, jnp.zeros_like(shaped)], axis=0)
    across = jnp.fft.fft(padded, axis=0)
    angle = angle_grid(jnp.arange(2 * blocks, dtype=jnp.int32), jnp.arange(P_SIZE, dtype=jnp.int32), 2 * LENGTH)
    turned = across * lax.complex(jnp.cos(angle), -jnp.sin(angle))[:, :, None]
    real_part = round_back(jnp.real(turned))
    other_part = round_back(jnp.imag(turned))
    return jnp.fft.fft(lax.complex(real_part, other_part), axis=1)

def untransform(spectrum, factor):
    blocks = LENGTH // P_SIZE
    width = spectrum.shape[2]
    within = jnp.fft.ifft(spectrum, axis=1) * P_SIZE
    angle = angle_grid(jnp.arange(2 * blocks, dtype=jnp.int32), jnp.arange(P_SIZE, dtype=jnp.int32), 2 * LENGTH)
    turned = within * lax.complex(jnp.cos(angle), jnp.sin(angle))[:, :, None]
    real_part = round_back(jnp.real(turned))
    other_part = round_back(jnp.imag(turned))
    across = jnp.fft.ifft(lax.complex(real_part, other_part), axis=0) * (2 * blocks)
    return (jnp.real(across[:blocks]) * factor).reshape(LENGTH, width).astype(jnp.bfloat16)

def channel_block(pieces):
    mixed, taps, gated = pieces
    mixed_spec = transform(mixed)
    taps_spec = transform(taps)
    gated_spec = transform(gated)
    scale = 1.0 / (2 * LENGTH)
    conv_out = untransform(mixed_spec * taps_spec, scale)
    back_grad = untransform(gated_spec * jnp.conj(taps_spec), scale)
    grad_filter = untransform(gated_spec * jnp.conj(mixed_spec), scale / math.sqrt(LENGTH))
    return (conv_out, back_grad, grad_filter)

def reference(layer_input, gate_query, gate_key, value_proj, grad_out, filter_taps):
    mixed = (gate_key.astype(jnp.float32) * value_proj.astype(jnp.float32)).astype(jnp.bfloat16)
    gated = (grad_out.astype(jnp.float32) * gate_query.astype(jnp.float32)).astype(jnp.bfloat16)
    group = math.gcd(D, 512)
    number = D // group

    def split_channels(array):
        return array.reshape(LENGTH, number, group).transpose(1, 0, 2)

    def join_channels(array):
        return array.transpose(1, 0, 2).reshape(LENGTH, D)
    conv_out, back_grad, grad_filter = lax.map(channel_block, (split_channels(mixed), split_channels(filter_taps), split_channels(gated)))
    conv_out = join_channels(conv_out)
    back_grad = join_channels(back_grad)
    grad_filter = join_channels(grad_filter)
    grad_query = (grad_out.astype(jnp.float32) * conv_out.astype(jnp.float32)).astype(jnp.bfloat16)
    grad_key = (back_grad.astype(jnp.float32) * value_proj.astype(jnp.float32)).astype(jnp.bfloat16)
    grad_value = (back_grad.astype(jnp.float32) * gate_key.astype(jnp.float32)).astype(jnp.bfloat16)
    grad_weight = jnp.dot(layer_input.T, grad_value, preferred_element_type=jnp.float32) * (1.0 / math.sqrt(LENGTH))
    return (grad_query, grad_key, grad_value, grad_filter, grad_weight)
```

```python
import math

import jax
import jax.numpy as jnp
import numpy as np
from jax import lax
from jax.sharding import PartitionSpec as P


def half_shift_table(span):
    step = (2 * np.arange(span)[:, None] + 1) * np.arange(span)[None, :] % (4 * span)
    angle = step * (2.0 * math.pi / (4 * span))
    return np.concatenate([np.cos(angle), -np.sin(angle)], axis=0).astype(jnp.bfloat16)


def product(ar, ai, br, bi):
    return ar * br - ai * bi, ar * bi + ai * br


def against(ar, ai, br, bi):
    return ar * br + ai * bi, ai * br - ar * bi


def phase_products(mixed, taps, gated, span):
    phases = mixed[0].shape[1]
    angle = (np.arange(span) + 0.5) * (math.pi / span)
    turn_cos = jnp.asarray(np.cos(angle), jnp.float32)[:, None]
    turn_sin = jnp.asarray(np.sin(angle), jnp.float32)[:, None]

    def at(pair, phase):
        return pair[0][:, phase], pair[1][:, phase]

    def total(terms):
        return sum(t[0] for t in terms), sum(t[1] for t in terms)

    def convolve(x, h, phase):
        near = [product(*at(x, a), *at(h, phase - a)) for a in range(phase + 1)]
        far = [product(*at(x, a), *at(h, phase - a + phases)) for a in range(phase + 1, phases)]
        out = total(near)
        if far:
            turned = product(*total(far), turn_cos, -turn_sin)
            out = total([out, turned])
        return out

    def correlate(g, h, phase):
        near = [against(*at(g, a), *at(h, a - phase)) for a in range(phase, phases)]
        far = [against(*at(g, a), *at(h, a - phase + phases)) for a in range(phase)]
        out = total(near)
        if far:
            turned = product(*total(far), turn_cos, turn_sin)
            out = total([out, turned])
        return out

    outs = []
    for rule, first, second in ((convolve, mixed, taps), (correlate, gated, taps), (correlate, gated, mixed)):
        parts = [rule(first, second, phase) for phase in range(phases)]
        real = jnp.stack([p[0] for p in parts], axis=1)
        other = jnp.stack([p[1] for p in parts], axis=1)
        outs.append((real, other))
    return outs


def times(first, second):
    return (first.astype(jnp.float32) * second.astype(jnp.float32)).astype(jnp.bfloat16)


def shards(layer_input, gate_query, gate_key, value_proj, grad_out, filter_taps):
    rows, width = gate_query.shape
    blocks = lax.axis_size("seq")
    length = rows * blocks
    share = width // blocks
    span = min(length, width)
    phases = length // span
    scale_root = 1.0 / math.sqrt(length)
    table = jnp.asarray(half_shift_table(span))

    features = lax.all_gather(layer_input, "chan", axis=1, tiled=True)
    mixed = times(gate_key, value_proj)
    gated = times(grad_out, gate_query)

    def cut(array):
        return array.reshape(rows, blocks, share).transpose(1, 0, 2)

    sent = jnp.stack([cut(mixed), cut(filter_taps), cut(gated), cut(gate_key)], axis=1)
    held = lax.all_to_all(sent, "seq", split_axis=0, concat_axis=0, tiled=True)
    whole = held.transpose(1, 0, 2, 3).reshape(4, length, share)
    signals = whole[:3].reshape(3, span, phases * share).transpose(1, 0, 2).reshape(span, -1)
    spectra = lax.dot_general(
        table, signals, (((1,), (0,)), ((), ())), preferred_element_type=jnp.float32
    ).reshape(2, span, 3, phases, share)
    pairs = [(spectra[0, :, s], spectra[1, :, s]) for s in range(3)]
    results = phase_products(*pairs, span)
    stacked = jnp.stack(
        [jnp.stack([r[0] for r in results], 1), jnp.stack([r[1] for r in results], 1)], 0
    ).astype(jnp.bfloat16)
    back = lax.dot_general(
        table,
        stacked.reshape(2 * span, 3 * phases * share),
        (((0,), (0,)), ((), ())),
        preferred_element_type=jnp.float32,
    ).reshape(span, 3, phases * share)
    weights = jnp.asarray([1.0, 1.0, scale_root], jnp.float32) / span
    back = (back * weights[None, :, None]).astype(jnp.bfloat16)
    back = back.transpose(1, 0, 2).reshape(3, length, share)
    value_all = lax.all_gather(times(back[1], whole[3]), "seq", axis=1, tiled=True)
    restored = lax.all_to_all(
        back.reshape(3, blocks, rows, share).transpose(1, 0, 2, 3),
        "seq", split_axis=0, concat_axis=0, tiled=True,
    ).transpose(1, 2, 0, 3).reshape(3, rows, width)
    columns = lax.all_to_all(features, "seq", split_axis=1, concat_axis=0, tiled=True)
    grad_weight = (
        lax.dot_general(
            columns, value_all, (((0,), (0,)), ((), ())), preferred_element_type=jnp.float32
        )
        * scale_root
    )
    return (
        times(grad_out, restored[0]),
        times(restored[1], value_proj),
        times(restored[1], gate_key),
        restored[2],
        grad_weight,
    )


def solution(mesh):
    spec = P("seq", "chan")
    return jax.shard_map(
        shards, mesh=mesh, in_specs=(spec,) * 6, out_specs=(spec,) * 5, check_vma=False
    )
```

```python
import functools
import math

import jax
import jax.numpy as jnp
import numpy as np
from jax import lax
from jax.experimental import pallas as pl
from jax.experimental.pallas import tpu as pltpu
from jax.sharding import PartitionSpec as P


def half_shift_table(span):
    step = (2 * np.arange(span)[:, None] + 1) * np.arange(span)[None, :] % (4 * span)
    angle = step * (2.0 * math.pi / (4 * span))
    return np.concatenate([np.cos(angle), -np.sin(angle)], axis=0).astype(jnp.bfloat16)


def product(ar, ai, br, bi):
    return ar * br - ai * bi, ar * bi + ai * br


def against(ar, ai, br, bi):
    return ar * br + ai * bi, ai * br - ar * bi


def phase_products(mixed, taps, gated, span):
    phases = mixed[0].shape[1]
    angle = (np.arange(span) + 0.5) * (math.pi / span)
    turn_cos = jnp.asarray(np.cos(angle), jnp.float32)[:, None]
    turn_sin = jnp.asarray(np.sin(angle), jnp.float32)[:, None]

    def at(pair, phase):
        return pair[0][:, phase], pair[1][:, phase]

    def total(terms):
        return sum(t[0] for t in terms), sum(t[1] for t in terms)

    def convolve(x, h, phase):
        near = [product(*at(x, a), *at(h, phase - a)) for a in range(phase + 1)]
        far = [product(*at(x, a), *at(h, phase - a + phases)) for a in range(phase + 1, phases)]
        out = total(near)
        if far:
            turned = product(*total(far), turn_cos, -turn_sin)
            out = total([out, turned])
        return out

    def correlate(g, h, phase):
        near = [against(*at(g, a), *at(h, a - phase)) for a in range(phase, phases)]
        far = [against(*at(g, a), *at(h, a - phase + phases)) for a in range(phase)]
        out = total(near)
        if far:
            turned = product(*total(far), turn_cos, turn_sin)
            out = total([out, turned])
        return out

    outs = []
    for rule, first, second in ((convolve, mixed, taps), (correlate, gated, taps), (correlate, gated, mixed)):
        parts = [rule(first, second, phase) for phase in range(phases)]
        real = jnp.stack([p[0] for p in parts], axis=1)
        other = jnp.stack([p[1] for p in parts], axis=1)
        outs.append((real, other))
    return outs


def times(first, second):
    return (first.astype(jnp.float32) * second.astype(jnp.float32)).astype(jnp.bfloat16)


def shards(layer_input, gate_query, gate_key, value_proj, grad_out, filter_taps):
    rows, width = gate_query.shape
    blocks = lax.axis_size("seq")
    length = rows * blocks
    share = width // blocks
    span = min(length, width)
    phases = length // span
    scale_root = 1.0 / math.sqrt(length)
    table = jnp.asarray(half_shift_table(span))

    features = lax.all_gather(layer_input, "chan", axis=1, tiled=True)
    mixed = times(gate_key, value_proj)
    gated = times(grad_out, gate_query)

    def cut(array):
        return array.reshape(rows, blocks, share).transpose(1, 0, 2)

    sent = jnp.stack([cut(mixed), cut(filter_taps), cut(gated), cut(gate_key)], axis=1)
    held = lax.all_to_all(sent, "seq", split_axis=0, concat_axis=0, tiled=True)
    whole = held.transpose(1, 0, 2, 3).reshape(4, length, share)
    signals = whole[:3].reshape(3, span, phases * share).transpose(1, 0, 2).reshape(span, -1)
    spectra = lax.dot_general(
        table, signals, (((1,), (0,)), ((), ())), preferred_element_type=jnp.float32
    ).reshape(2, span, 3, phases, share)
    pairs = [(spectra[0, :, s], spectra[1, :, s]) for s in range(3)]
    results = phase_products(*pairs, span)
    stacked = jnp.stack(
        [jnp.stack([r[0] for r in results], 1), jnp.stack([r[1] for r in results], 1)], 0
    ).astype(jnp.bfloat16)
    back = lax.dot_general(
        table,
        stacked.reshape(2 * span, 3 * phases * share),
        (((0,), (0,)), ((), ())),
        preferred_element_type=jnp.float32,
    ).reshape(span, 3, phases * share)
    weights = jnp.asarray([1.0, 1.0, scale_root], jnp.float32) / span
    back = (back * weights[None, :, None]).astype(jnp.bfloat16)
    back = back.transpose(1, 0, 2).reshape(3, length, share)
    value_all = lax.all_gather(times(back[1], whole[3]), "seq", axis=1, tiled=True)
    restored = lax.all_to_all(
        back.reshape(3, blocks, rows, share).transpose(1, 0, 2, 3),
        "seq", split_axis=0, concat_axis=0, tiled=True,
    ).transpose(1, 2, 0, 3).reshape(3, rows, width)
    columns = lax.all_to_all(features, "seq", split_axis=1, concat_axis=0, tiled=True)
    grad_weight = (
        lax.dot_general(
            columns, value_all, (((0,), (0,)), ((), ())), preferred_element_type=jnp.float32
        )
        * scale_root
    )
    return (
        times(grad_out, restored[0]),
        times(restored[1], value_proj),
        times(restored[1], gate_key),
        restored[2],
        grad_weight,
    )


def fused_kernel(
    blocks, groups, scale_root,
    layer, query, key, value, cotangent, taps, forward_hbm, inverse_hbm,
    out_query, out_key, out_value, out_filter, out_weight,
    send, recv, feats, columns, columns_t, prods, own_value, res, rest, values, forward, inverse,
    sig_send, sig_recv, chan_send, chan_recv, col_send, col_recv,
    res_send, res_recv, val_send, val_recv, fwd_send, fwd_recv, local_sem,
):
    rows, width = key.shape
    share = width // blocks
    span = rows * blocks
    held = columns.shape[1]
    chips = blocks // 2
    me = lax.axis_index("seq")
    group = lax.axis_index("chan")
    chip = me // 2
    core = me % 2
    sibling = me + 1 - 2 * core

    def lanes(index, size=share):
        return pl.ds(pl.multiple_of(index * size, size), size)

    def block_rows(index):
        return pl.ds(pl.multiple_of(index * rows, rows), rows)

    def remote(source, target, sends, recvs, slot, device):
        return pltpu.make_async_remote_copy(
            src_ref=source, dst_ref=target, send_sem=sends.at[slot], recv_sem=recvs.at[slot],
            device_id=device, device_id_type=pl.DeviceIdType.MESH,
        )

    barrier = pltpu.get_barrier_semaphore()
    for d in range(1, blocks):
        pl.semaphore_signal(barrier, inc=1, device_id={"seq": (me + d) % blocks},
                            device_id_type=pl.DeviceIdType.MESH)
    for d in range(1, groups):
        pl.semaphore_signal(barrier, inc=1, device_id={"chan": (group + d) % groups},
                            device_id_type=pl.DeviceIdType.MESH)
    tables = [
        pltpu.make_async_copy(forward_hbm, forward, local_sem.at[0]),
        pltpu.make_async_copy(inverse_hbm, inverse, local_sem.at[1]),
    ]
    for copy in tables:
        copy.start()
    send[0] = times(key[...], value[...])
    send[1] = taps[...]
    send[2] = times(cotangent[...], query[...])
    send[3] = key[...]
    pl.semaphore_wait(barrier, blocks + groups - 2)

    signals = []
    for d in range(1, blocks):
        peer = (me + d) % blocks
        copy = remote(send.at[:, :, lanes(peer)], recv.at[:, block_rows(me), :],
                      sig_send, sig_recv, d - 1, {"seq": peer})
        copy.start()
        signals.append(copy)
    gathers = []
    for d in range(1, groups):
        copy = remote(layer, feats.at[group], chan_send, chan_recv, d - 1,
                      {"chan": (group + d) % groups})
        copy.start()
        gathers.append(copy)
    own_signal = pltpu.make_async_copy(
        send.at[:, :, lanes(me)], recv.at[:, block_rows(me), :], local_sem.at[2])
    own_signal.start()
    own_layer = pltpu.make_async_copy(layer, feats.at[group], local_sem.at[3])
    own_layer.start()

    for copy in tables:
        copy.wait()
    own_signal.wait()
    own_layer.wait()
    for copy in signals:
        copy.wait_recv()

    tile = 2 * rows

    def forward_step(index, carry):
        low = pl.ds(pl.multiple_of(index * tile, tile), tile)
        high = pl.ds(pl.multiple_of(span + index * tile, tile), tile)
        operand = jnp.concatenate([recv[0], recv[1], recv[2]], axis=1)
        real = jnp.dot(forward[low, :], operand, preferred_element_type=jnp.float32)
        other = jnp.dot(forward[high, :], operand, preferred_element_type=jnp.float32)
        m, h, g = [(real[:, i * share : (i + 1) * share], other[:, i * share : (i + 1) * share])
                   for i in range(3)]
        for i, pair in enumerate((product(*m, *h), against(*g, *h), against(*g, *m))):
            prods[low, i * share : (i + 1) * share] = pair[0].astype(jnp.bfloat16)
            prods[high, i * share : (i + 1) * share] = pair[1].astype(jnp.bfloat16)
        return carry

    lax.fori_loop(0, span // tile, forward_step, 0)

    for copy in gathers:
        copy.wait_recv()

    def feature_block(index):
        return feats.at[index * held // width, :,
                        pl.ds(pl.multiple_of(index * held % width, held), held)]

    sent_columns = []
    for d in range(1, blocks):
        peer = (me + d) % blocks
        copy = remote(feature_block(peer), columns.at[block_rows(me), :],
                      col_send, col_recv, d - 1, {"seq": peer})
        copy.start()
        sent_columns.append(copy)
    own_columns = pltpu.make_async_copy(
        feature_block(me), columns.at[block_rows(me), :], local_sem.at[4])
    own_columns.start()

    def inverse_step(index, carry):
        part = pl.ds(pl.multiple_of(index * tile, tile), tile)
        total = jnp.dot(inverse[part, :], prods[...], preferred_element_type=jnp.float32)
        total = total * (1.0 / span)
        res[0, part, :] = total[:, :share].astype(jnp.bfloat16)
        back = total[:, share : 2 * share].astype(jnp.bfloat16)
        res[1, part, :] = back
        res[2, part, :] = (total[:, 2 * share :] * scale_root).astype(jnp.bfloat16)
        own_value[part, :] = times(back, recv[3, part, :])
        return carry

    lax.fori_loop(0, span // tile, inverse_step, 0)

    sent_values = []
    for d in range(1, chips):
        peer = 2 * ((chip + d) % chips) + core
        copy = remote(own_value, values.at[:, lanes(me)], val_send, val_recv, d - 1, {"seq": peer})
        copy.start()
        sent_values.append(copy)
    copy = remote(own_value, values.at[:, lanes(me)], val_send, val_recv, chips - 1,
                  {"seq": sibling})
    copy.start()
    sent_values.append(copy)
    results = []
    for d in range(1, blocks):
        peer = (me + d) % blocks
        copy = remote(res.at[:, block_rows(peer), :], rest.at[:, :, lanes(me)],
                      res_send, res_recv, d - 1, {"seq": peer})
        copy.start()
        results.append(copy)
    own_result = pltpu.make_async_copy(
        res.at[:, block_rows(me), :], rest.at[:, :, lanes(me)], local_sem.at[5])
    own_result.start()
    own_column_value = pltpu.make_async_copy(own_value, values.at[:, lanes(me)], local_sem.at[6])
    own_column_value.start()

    own_columns.wait()
    for copy in sent_columns:
        copy.wait_recv()

    def turn_step(index, carry):
        part = pl.ds(pl.multiple_of(index * rows, rows), rows)
        columns_t[:, part] = columns[part, :].T
        return carry

    lax.fori_loop(0, blocks, turn_step, 0)

    passed_on = []
    for d in range(1, chips):
        sent_values[d - 1].wait_recv()
        origin = 2 * ((chip + chips - d) % chips) + core
        copy = remote(values.at[:, lanes(origin)], values.at[:, lanes(origin)],
                      fwd_send, fwd_recv, d - 1, {"seq": sibling})
        copy.start()
        passed_on.append(copy)

    own_result.wait()
    for copy in results:
        copy.wait_recv()
    out_query[...] = times(cotangent[...], rest[0])
    out_key[...] = times(rest[1], value[...])
    out_value[...] = times(rest[1], key[...])
    out_filter[...] = rest[2]

    own_column_value.wait()
    sent_values[chips - 1].wait_recv()
    for copy in passed_on:
        copy.wait_recv()

    wide = 2 * share

    def weight_step(index, carry):
        part = lanes(index, wide)
        out_weight[:, part] = scale_root * jnp.dot(
            columns_t[...], values[:, part], preferred_element_type=jnp.float32)
        return carry

    lax.fori_loop(0, width // wide, weight_step, 0)
    for copy in signals + gathers + sent_columns + sent_values + results + passed_on:
        copy.wait_send()


def fused(layer_input, gate_query, gate_key, value_proj, grad_out, filter_taps):
    rows, width = gate_query.shape
    blocks = lax.axis_size("seq")
    groups = lax.axis_size("chan")
    length = rows * blocks
    share = width // blocks
    held = width * groups // blocks
    table = half_shift_table(length)
    kind = gate_query.dtype
    vmem = pl.BlockSpec(memory_space=pltpu.VMEM)
    hbm = pl.BlockSpec(memory_space=pl.ANY)
    dma = pltpu.SemaphoreType.DMA
    signal = jax.ShapeDtypeStruct((rows, width), kind)
    return pl.pallas_call(
        functools.partial(fused_kernel, blocks, groups, 1.0 / math.sqrt(length)),
        out_shape=[signal] * 4 + [jax.ShapeDtypeStruct((held, width), jnp.float32)],
        in_specs=[vmem] * 6 + [hbm] * 2,
        out_specs=[vmem] * 5,
        scratch_shapes=[
            pltpu.VMEM((4, rows, width), kind),
            pltpu.VMEM((4, length, share), kind),
            pltpu.VMEM((groups, rows, width), kind),
            pltpu.VMEM((length, held), kind),
            pltpu.VMEM((held, length), kind),
            pltpu.VMEM((2 * length, 3 * share), kind),
            pltpu.VMEM((length, share), kind),
            pltpu.VMEM((3, length, share), kind),
            pltpu.VMEM((3, rows, width), kind),
            pltpu.VMEM((length, width), kind),
            pltpu.VMEM((2 * length, length), kind),
            pltpu.VMEM((length, 2 * length), kind),
            dma((blocks - 1,)), dma((blocks - 1,)),
            dma((groups,)), dma((groups,)),
            dma((blocks - 1,)), dma((blocks - 1,)),
            dma((blocks - 1,)), dma((blocks - 1,)),
            dma((blocks // 2,)), dma((blocks // 2,)),
            dma((blocks // 2,)), dma((blocks // 2,)),
            dma((8,)),
        ],
        compiler_params=pltpu.CompilerParams(
            collective_id=0, has_side_effects=True, vmem_limit_bytes=48 * 2**20
        ),
    )(layer_input, gate_query, gate_key, value_proj, grad_out, filter_taps,
      jnp.asarray(table), jnp.asarray(np.ascontiguousarray(table.T)))


def body(*arrays):
    rows, width = arrays[1].shape
    blocks = lax.axis_size("seq")
    share = width // blocks
    if share % 128 == 0 and rows % 16 == 0 and blocks % 2 == 0 and rows * blocks <= width:
        return tuple(fused(*arrays))
    return shards(*arrays)


def solution(mesh):
    spec = P("seq", "chan")
    return jax.shard_map(
        body, mesh=mesh, in_specs=(spec,) * 6, out_specs=(spec,) * 5, check_vma=False
    )
```

```python
import functools
import math

import jax
import jax.numpy as jnp
import numpy as np
from jax import lax
from jax.experimental import pallas as pl
from jax.experimental.pallas import tpu as pltpu
from jax.sharding import PartitionSpec as P


def half_shift_table(span):
    step = (2 * np.arange(span)[:, None] + 1) * np.arange(span)[None, :] % (4 * span)
    angle = step * (2.0 * math.pi / (4 * span))
    return np.concatenate([np.cos(angle), -np.sin(angle)], axis=0).astype(jnp.bfloat16)


def product(ar, ai, br, bi):
    return ar * br - ai * bi, ar * bi + ai * br


def against(ar, ai, br, bi):
    return ar * br + ai * bi, ai * br - ar * bi


def phase_products(mixed, taps, gated, span):
    phases = mixed[0].shape[1]
    angle = (np.arange(span) + 0.5) * (math.pi / span)
    turn_cos = jnp.asarray(np.cos(angle), jnp.float32)[:, None]
    turn_sin = jnp.asarray(np.sin(angle), jnp.float32)[:, None]

    def at(pair, phase):
        return pair[0][:, phase], pair[1][:, phase]

    def total(terms):
        return sum(t[0] for t in terms), sum(t[1] for t in terms)

    def convolve(x, h, phase):
        near = [product(*at(x, a), *at(h, phase - a)) for a in range(phase + 1)]
        far = [product(*at(x, a), *at(h, phase - a + phases)) for a in range(phase + 1, phases)]
        out = total(near)
        if far:
            turned = product(*total(far), turn_cos, -turn_sin)
            out = total([out, turned])
        return out

    def correlate(g, h, phase):
        near = [against(*at(g, a), *at(h, a - phase)) for a in range(phase, phases)]
        far = [against(*at(g, a), *at(h, a - phase + phases)) for a in range(phase)]
        out = total(near)
        if far:
            turned = product(*total(far), turn_cos, turn_sin)
            out = total([out, turned])
        return out

    outs = []
    for rule, first, second in ((convolve, mixed, taps), (correlate, gated, taps), (correlate, gated, mixed)):
        parts = [rule(first, second, phase) for phase in range(phases)]
        real = jnp.stack([p[0] for p in parts], axis=1)
        other = jnp.stack([p[1] for p in parts], axis=1)
        outs.append((real, other))
    return outs


def times(first, second):
    return (first.astype(jnp.float32) * second.astype(jnp.float32)).astype(jnp.bfloat16)


def shards(layer_input, gate_query, gate_key, value_proj, grad_out, filter_taps):
    rows, width = gate_query.shape
    blocks = lax.axis_size("seq")
    length = rows * blocks
    share = width // blocks
    span = min(length, width)
    phases = length // span
    scale_root = 1.0 / math.sqrt(length)
    table = jnp.asarray(half_shift_table(span))

    features = lax.all_gather(layer_input, "chan", axis=1, tiled=True)
    mixed = times(gate_key, value_proj)
    gated = times(grad_out, gate_query)

    def cut(array):
        return array.reshape(rows, blocks, share).transpose(1, 0, 2)

    sent = jnp.stack([cut(mixed), cut(filter_taps), cut(gated), cut(gate_key)], axis=1)
    held = lax.all_to_all(sent, "seq", split_axis=0, concat_axis=0, tiled=True)
    whole = held.transpose(1, 0, 2, 3).reshape(4, length, share)
    signals = whole[:3].reshape(3, span, phases * share).transpose(1, 0, 2).reshape(span, -1)
    spectra = lax.dot_general(
        table, signals, (((1,), (0,)), ((), ())), preferred_element_type=jnp.float32
    ).reshape(2, span, 3, phases, share)
    pairs = [(spectra[0, :, s], spectra[1, :, s]) for s in range(3)]
    results = phase_products(*pairs, span)
    stacked = jnp.stack(
        [jnp.stack([r[0] for r in results], 1), jnp.stack([r[1] for r in results], 1)], 0
    ).astype(jnp.bfloat16)
    back = lax.dot_general(
        table,
        stacked.reshape(2 * span, 3 * phases * share),
        (((0,), (0,)), ((), ())),
        preferred_element_type=jnp.float32,
    ).reshape(span, 3, phases * share)
    weights = jnp.asarray([1.0, 1.0, scale_root], jnp.float32) / span
    back = (back * weights[None, :, None]).astype(jnp.bfloat16)
    back = back.transpose(1, 0, 2).reshape(3, length, share)
    value_all = lax.all_gather(times(back[1], whole[3]), "seq", axis=1, tiled=True)
    restored = lax.all_to_all(
        back.reshape(3, blocks, rows, share).transpose(1, 0, 2, 3),
        "seq", split_axis=0, concat_axis=0, tiled=True,
    ).transpose(1, 2, 0, 3).reshape(3, rows, width)
    columns = lax.all_to_all(features, "seq", split_axis=1, concat_axis=0, tiled=True)
    grad_weight = (
        lax.dot_general(
            columns, value_all, (((0,), (0,)), ((), ())), preferred_element_type=jnp.float32
        )
        * scale_root
    )
    return (
        times(grad_out, restored[0]),
        times(restored[1], value_proj),
        times(restored[1], gate_key),
        restored[2],
        grad_weight,
    )


def fused_kernel(
    blocks, groups, scale_root,
    layer_hbm, query_hbm, key_hbm, value_hbm, cotangent_hbm, taps_hbm, forward_hbm, inverse_hbm,
    out_query, out_key, out_value, out_filter, out_weight,
    layer, query, key, value, cotangent, taps,
    send, recv, feats, columns, columns_t, prods, own_value, res, rest, values, forward, inverse,
    sig_send, sig_recv, chan_send, chan_recv, col_send, col_recv,
    res_send, res_recv, val_send, val_recv, fwd_send, fwd_recv, local_sem, in_sem,
):
    rows, width = key_hbm.shape
    share = width // blocks
    span = rows * blocks
    held = columns.shape[1]
    chips = blocks // 2
    me = lax.axis_index("seq")
    group = lax.axis_index("chan")
    chip = me // 2
    core = me % 2
    sibling = me + 1 - 2 * core

    def lanes(index, size=share):
        return pl.ds(pl.multiple_of(index * size, size), size)

    def block_rows(index):
        return pl.ds(pl.multiple_of(index * rows, rows), rows)

    def remote(source, target, sends, recvs, slot, device):
        return pltpu.make_async_remote_copy(
            src_ref=source, dst_ref=target, send_sem=sends.at[slot], recv_sem=recvs.at[slot],
            device_id=device, device_id_type=pl.DeviceIdType.MESH,
        )

    inputs = [
        pltpu.make_async_copy(source, target, in_sem.at[i])
        for i, (source, target) in enumerate((
            (key_hbm, key), (value_hbm, value), (cotangent_hbm, cotangent),
            (query_hbm, query), (taps_hbm, taps), (layer_hbm, layer)))
    ]
    for copy in inputs:
        copy.start()
    barrier = pltpu.get_barrier_semaphore()
    for d in range(1, blocks):
        pl.semaphore_signal(barrier, inc=1, device_id={"seq": (me + d) % blocks},
                            device_id_type=pl.DeviceIdType.MESH)
    for d in range(1, groups):
        pl.semaphore_signal(barrier, inc=1, device_id={"chan": (group + d) % groups},
                            device_id_type=pl.DeviceIdType.MESH)
    tables = [
        pltpu.make_async_copy(forward_hbm, forward, local_sem.at[0]),
        pltpu.make_async_copy(inverse_hbm, inverse, local_sem.at[1]),
    ]
    for copy in tables:
        copy.start()
    for copy in inputs:
        copy.wait()
    send[0] = times(key[...], value[...])
    send[1] = taps[...]
    send[2] = times(cotangent[...], query[...])
    send[3] = key[...]
    pl.semaphore_wait(barrier, blocks + groups - 2)

    signals = []
    for d in range(1, blocks):
        peer = (me + d) % blocks
        copy = remote(send.at[:, :, lanes(peer)], recv.at[:, block_rows(me), :],
                      sig_send, sig_recv, d - 1, {"seq": peer})
        copy.start()
        signals.append(copy)
    gathers = []
    for d in range(1, groups):
        copy = remote(layer, feats.at[group], chan_send, chan_recv, d - 1,
                      {"chan": (group + d) % groups})
        copy.start()
        gathers.append(copy)
    own_signal = pltpu.make_async_copy(
        send.at[:, :, lanes(me)], recv.at[:, block_rows(me), :], local_sem.at[2])
    own_signal.start()
    own_layer = pltpu.make_async_copy(layer, feats.at[group], local_sem.at[3])
    own_layer.start()

    for copy in tables:
        copy.wait()
    own_signal.wait()
    own_layer.wait()
    for copy in signals:
        copy.wait_recv()

    tile = 2 * rows

    def forward_step(index, carry):
        low = pl.ds(pl.multiple_of(index * tile, tile), tile)
        high = pl.ds(pl.multiple_of(span + index * tile, tile), tile)
        operand = jnp.concatenate([recv[0], recv[1], recv[2]], axis=1)
        real = jnp.dot(forward[low, :], operand, preferred_element_type=jnp.float32)
        other = jnp.dot(forward[high, :], operand, preferred_element_type=jnp.float32)
        m, h, g = [(real[:, i * share : (i + 1) * share], other[:, i * share : (i + 1) * share])
                   for i in range(3)]
        for i, pair in enumerate((product(*m, *h), against(*g, *h), against(*g, *m))):
            prods[low, i * share : (i + 1) * share] = pair[0].astype(jnp.bfloat16)
            prods[high, i * share : (i + 1) * share] = pair[1].astype(jnp.bfloat16)
        return carry

    lax.fori_loop(0, span // tile, forward_step, 0)

    for copy in gathers:
        copy.wait_recv()

    def feature_block(index):
        return feats.at[index * held // width, :,
                        pl.ds(pl.multiple_of(index * held % width, held), held)]

    sent_columns = []
    for d in range(1, blocks):
        peer = (me + d) % blocks
        copy = remote(feature_block(peer), columns.at[block_rows(me), :],
                      col_send, col_recv, d - 1, {"seq": peer})
        copy.start()
        sent_columns.append(copy)
    own_columns = pltpu.make_async_copy(
        feature_block(me), columns.at[block_rows(me), :], local_sem.at[4])
    own_columns.start()

    def inverse_step(index, carry):
        part = pl.ds(pl.multiple_of(index * tile, tile), tile)
        total = jnp.dot(inverse[part, :], prods[...], preferred_element_type=jnp.float32)
        total = total * (1.0 / span)
        res[0, part, :] = total[:, :share].astype(jnp.bfloat16)
        back = total[:, share : 2 * share].astype(jnp.bfloat16)
        res[1, part, :] = back
        res[2, part, :] = (total[:, 2 * share :] * scale_root).astype(jnp.bfloat16)
        own_value[part, :] = times(back, recv[3, part, :])
        return carry

    halves = [pl.ds(0, span // 2), pl.ds(span // 2, span // 2)]
    steps = span // tile // 2
    sent_values = []
    for half, part in enumerate(halves):
        lax.fori_loop(half * steps, half * steps + steps, inverse_step, 0)
        for d in range(1, chips + 1):
            peer = 2 * ((chip + d) % chips) + core if d < chips else sibling
            copy = remote(own_value.at[part, :], values.at[part, lanes(me)],
                          val_send, val_recv, half * chips + d - 1, {"seq": peer})
            copy.start()
            sent_values.append(copy)
    results = []
    for d in range(1, blocks):
        peer = (me + d) % blocks
        copy = remote(res.at[:, block_rows(peer), :], rest.at[:, :, lanes(me)],
                      res_send, res_recv, d - 1, {"seq": peer})
        copy.start()
        results.append(copy)
    own_result = pltpu.make_async_copy(
        res.at[:, block_rows(me), :], rest.at[:, :, lanes(me)], local_sem.at[5])
    own_result.start()
    own_column_value = pltpu.make_async_copy(own_value, values.at[:, lanes(me)], local_sem.at[6])
    own_column_value.start()

    own_columns.wait()
    for copy in sent_columns:
        copy.wait_recv()

    def turn_step(index, carry):
        part = pl.ds(pl.multiple_of(index * rows, rows), rows)
        columns_t[:, part] = columns[part, :].T
        return carry

    lax.fori_loop(0, blocks, turn_step, 0)

    wide = 2 * share

    def weigh(index):
        part = lanes(index, wide)
        out_weight[:, part] = scale_root * jnp.dot(
            columns_t[...], values[:, part], preferred_element_type=jnp.float32)

    passed_on = []
    for half, part in enumerate(halves):
        for d in range(1, chips):
            sent_values[half * chips + d - 1].wait_recv()
            block = values.at[part, lanes(2 * ((chip + chips - d) % chips) + core)]
            copy = remote(block, block, fwd_send, fwd_recv, half * chips + d - 1,
                          {"seq": sibling})
            copy.start()
            passed_on.append(copy)

    own_column_value.wait()
    for half in range(2):
        sent_values[half * chips + chips - 1].wait_recv()
    weigh(chip)
    for d in range(1, chips):
        for half in range(2):
            passed_on[half * (chips - 1) + d - 1].wait_recv()
        weigh((chip + chips - d) % chips)

    own_result.wait()
    for copy in results:
        copy.wait_recv()
    out_query[...] = times(cotangent[...], rest[0])
    out_key[...] = times(rest[1], value[...])
    out_value[...] = times(rest[1], key[...])
    out_filter[...] = rest[2]
    for copy in signals + gathers + sent_columns + sent_values + results + passed_on:
        copy.wait_send()


def fused(layer_input, gate_query, gate_key, value_proj, grad_out, filter_taps):
    rows, width = gate_query.shape
    blocks = lax.axis_size("seq")
    groups = lax.axis_size("chan")
    length = rows * blocks
    share = width // blocks
    held = width * groups // blocks
    table = half_shift_table(length)
    kind = gate_query.dtype
    vmem = pl.BlockSpec(memory_space=pltpu.VMEM)
    hbm = pl.BlockSpec(memory_space=pltpu.HBM)
    dma = pltpu.SemaphoreType.DMA
    signal = jax.ShapeDtypeStruct((rows, width), kind)
    return pl.pallas_call(
        functools.partial(fused_kernel, blocks, groups, 1.0 / math.sqrt(length)),
        out_shape=[signal] * 4 + [jax.ShapeDtypeStruct((held, width), jnp.float32)],
        in_specs=[hbm] * 8,
        out_specs=[vmem] * 5,
        scratch_shapes=[pltpu.VMEM((rows, width), kind)] * 6 + [
            pltpu.VMEM((4, rows, width), kind),
            pltpu.VMEM((4, length, share), kind),
            pltpu.VMEM((groups, rows, width), kind),
            pltpu.VMEM((length, held), kind),
            pltpu.VMEM((held, length), kind),
            pltpu.VMEM((2 * length, 3 * share), kind),
            pltpu.VMEM((length, share), kind),
            pltpu.VMEM((3, length, share), kind),
            pltpu.VMEM((3, rows, width), kind),
            pltpu.VMEM((length, width), kind),
            pltpu.VMEM((2 * length, length), kind),
            pltpu.VMEM((length, 2 * length), kind),
            dma((blocks - 1,)), dma((blocks - 1,)),
            dma((groups,)), dma((groups,)),
            dma((blocks - 1,)), dma((blocks - 1,)),
            dma((blocks - 1,)), dma((blocks - 1,)),
            dma((blocks,)), dma((blocks,)),
            dma((blocks,)), dma((blocks,)),
            dma((8,)), dma((6,)),
        ],
        compiler_params=pltpu.CompilerParams(
            collective_id=0, has_side_effects=True, vmem_limit_bytes=63 * 2**20
        ),
    )(layer_input, gate_query, gate_key, value_proj, grad_out, filter_taps,
      jnp.asarray(table), jnp.asarray(np.ascontiguousarray(table.T)))


def body(*arrays):
    rows, width = arrays[1].shape
    blocks = lax.axis_size("seq")
    share = width // blocks
    if share % 128 == 0 and rows % 16 == 0 and blocks % 2 == 0 and rows * blocks <= width:
        return tuple(fused(*arrays))
    return shards(*arrays)


def solution(mesh):
    spec = P("seq", "chan")
    return jax.shard_map(
        body, mesh=mesh, in_specs=(spec,) * 6, out_specs=(spec,) * 5, check_vma=False
    )
```

```python
import functools
import math

import jax
import jax.numpy as jnp
import numpy as np
from jax import lax
from jax.experimental import pallas as pl
from jax.experimental.pallas import tpu as pltpu
from jax.sharding import PartitionSpec as P


def half_shift_table(span):
    step = (2 * np.arange(span)[:, None] + 1) * np.arange(span)[None, :] % (4 * span)
    angle = step * (2.0 * math.pi / (4 * span))
    return np.concatenate([np.cos(angle), -np.sin(angle)], axis=0).astype(jnp.bfloat16)


def product(ar, ai, br, bi):
    return ar * br - ai * bi, ar * bi + ai * br


def against(ar, ai, br, bi):
    return ar * br + ai * bi, ai * br - ar * bi


def phase_products(mixed, taps, gated, span):
    phases = mixed[0].shape[1]
    angle = (np.arange(span) + 0.5) * (math.pi / span)
    turn_cos = jnp.asarray(np.cos(angle), jnp.float32)[:, None]
    turn_sin = jnp.asarray(np.sin(angle), jnp.float32)[:, None]

    def at(pair, phase):
        return pair[0][:, phase], pair[1][:, phase]

    def total(terms):
        return sum(t[0] for t in terms), sum(t[1] for t in terms)

    def convolve(x, h, phase):
        near = [product(*at(x, a), *at(h, phase - a)) for a in range(phase + 1)]
        far = [product(*at(x, a), *at(h, phase - a + phases)) for a in range(phase + 1, phases)]
        out = total(near)
        if far:
            turned = product(*total(far), turn_cos, -turn_sin)
            out = total([out, turned])
        return out

    def correlate(g, h, phase):
        near = [against(*at(g, a), *at(h, a - phase)) for a in range(phase, phases)]
        far = [against(*at(g, a), *at(h, a - phase + phases)) for a in range(phase)]
        out = total(near)
        if far:
            turned = product(*total(far), turn_cos, turn_sin)
            out = total([out, turned])
        return out

    outs = []
    for rule, first, second in ((convolve, mixed, taps), (correlate, gated, taps), (correlate, gated, mixed)):
        parts = [rule(first, second, phase) for phase in range(phases)]
        real = jnp.stack([p[0] for p in parts], axis=1)
        other = jnp.stack([p[1] for p in parts], axis=1)
        outs.append((real, other))
    return outs


def times(first, second):
    return (first.astype(jnp.float32) * second.astype(jnp.float32)).astype(jnp.bfloat16)


def shards(layer_input, gate_query, gate_key, value_proj, grad_out, filter_taps):
    rows, width = gate_query.shape
    blocks = lax.axis_size("seq")
    length = rows * blocks
    share = width // blocks
    span = min(length, width)
    phases = length // span
    scale_root = 1.0 / math.sqrt(length)
    table = jnp.asarray(half_shift_table(span))

    features = lax.all_gather(layer_input, "chan", axis=1, tiled=True)
    mixed = times(gate_key, value_proj)
    gated = times(grad_out, gate_query)

    def cut(array):
        return array.reshape(rows, blocks, share).transpose(1, 0, 2)

    sent = jnp.stack([cut(mixed), cut(filter_taps), cut(gated), cut(gate_key)], axis=1)
    held = lax.all_to_all(sent, "seq", split_axis=0, concat_axis=0, tiled=True)
    whole = held.transpose(1, 0, 2, 3).reshape(4, length, share)
    signals = whole[:3].reshape(3, span, phases * share).transpose(1, 0, 2).reshape(span, -1)
    spectra = lax.dot_general(
        table, signals, (((1,), (0,)), ((), ())), preferred_element_type=jnp.float32
    ).reshape(2, span, 3, phases, share)
    pairs = [(spectra[0, :, s], spectra[1, :, s]) for s in range(3)]
    results = phase_products(*pairs, span)
    stacked = jnp.stack(
        [jnp.stack([r[0] for r in results], 1), jnp.stack([r[1] for r in results], 1)], 0
    ).astype(jnp.bfloat16)
    back = lax.dot_general(
        table,
        stacked.reshape(2 * span, 3 * phases * share),
        (((0,), (0,)), ((), ())),
        preferred_element_type=jnp.float32,
    ).reshape(span, 3, phases * share)
    weights = jnp.asarray([1.0, 1.0, scale_root], jnp.float32) / span
    back = (back * weights[None, :, None]).astype(jnp.bfloat16)
    back = back.transpose(1, 0, 2).reshape(3, length, share)
    value_all = lax.all_gather(times(back[1], whole[3]), "seq", axis=1, tiled=True)
    restored = lax.all_to_all(
        back.reshape(3, blocks, rows, share).transpose(1, 0, 2, 3),
        "seq", split_axis=0, concat_axis=0, tiled=True,
    ).transpose(1, 2, 0, 3).reshape(3, rows, width)
    columns = lax.all_to_all(features, "seq", split_axis=1, concat_axis=0, tiled=True)
    grad_weight = (
        lax.dot_general(
            columns, value_all, (((0,), (0,)), ((), ())), preferred_element_type=jnp.float32
        )
        * scale_root
    )
    return (
        times(grad_out, restored[0]),
        times(restored[1], value_proj),
        times(restored[1], gate_key),
        restored[2],
        grad_weight,
    )


def fused_kernel(
    blocks, groups, scale_root,
    layer_hbm, query_hbm, key_hbm, value_hbm, cotangent_hbm, taps_hbm, forward_hbm, inverse_hbm,
    out_query, out_key, out_value, out_filter, out_weight,
    layer, query, key, value, cotangent, taps,
    send, recv, feats, columns, columns_t, prods, own_value, res, rest, values, forward, inverse,
    sig_send, sig_recv, chan_send, chan_recv, col_send, col_recv,
    res_send, res_recv, val_send, val_recv, fwd_send, fwd_recv, local_sem, in_sem,
):
    rows, width = key_hbm.shape
    share = width // blocks
    span = rows * blocks
    held = columns.shape[1]
    chips = blocks // 2
    me = lax.axis_index("seq")
    group = lax.axis_index("chan")
    chip = me // 2
    core = me % 2
    sibling = me + 1 - 2 * core

    def lanes(index, size=share):
        return pl.ds(pl.multiple_of(index * size, size), size)

    def block_rows(index):
        return pl.ds(pl.multiple_of(index * rows, rows), rows)

    def remote(source, target, sends, recvs, slot, device):
        return pltpu.make_async_remote_copy(
            src_ref=source, dst_ref=target, send_sem=sends.at[slot], recv_sem=recvs.at[slot],
            device_id=device, device_id_type=pl.DeviceIdType.MESH,
        )

    inputs = [
        pltpu.make_async_copy(source, target, in_sem.at[i])
        for i, (source, target) in enumerate((
            (key_hbm, key), (value_hbm, value), (cotangent_hbm, cotangent),
            (query_hbm, query), (taps_hbm, taps), (layer_hbm, layer)))
    ]
    for copy in inputs:
        copy.start()
    barrier = pltpu.get_barrier_semaphore()
    for d in range(1, blocks):
        pl.semaphore_signal(barrier, inc=1, device_id={"seq": (me + d) % blocks},
                            device_id_type=pl.DeviceIdType.MESH)
    for d in range(1, groups):
        pl.semaphore_signal(barrier, inc=1, device_id={"chan": (group + d) % groups},
                            device_id_type=pl.DeviceIdType.MESH)
    tables = [
        pltpu.make_async_copy(forward_hbm, forward, local_sem.at[0]),
        pltpu.make_async_copy(inverse_hbm, inverse, local_sem.at[1]),
    ]
    for copy in tables:
        copy.start()
    for copy in inputs:
        copy.wait()
    send[0] = times(key[...], value[...])
    send[1] = taps[...]
    send[2] = times(cotangent[...], query[...])
    send[3] = key[...]
    pl.semaphore_wait(barrier, blocks + groups - 2)

    signals = []
    for d in range(1, blocks):
        peer = (me + d) % blocks
        copy = remote(send.at[:, :, lanes(peer)], recv.at[:, block_rows(me), :],
                      sig_send, sig_recv, d - 1, {"seq": peer})
        copy.start()
        signals.append(copy)
    gathers = []
    for d in range(1, groups):
        copy = remote(layer, feats.at[group], chan_send, chan_recv, d - 1,
                      {"chan": (group + d) % groups})
        copy.start()
        gathers.append(copy)
    own_signal = pltpu.make_async_copy(
        send.at[:, :, lanes(me)], recv.at[:, block_rows(me), :], local_sem.at[2])
    own_signal.start()
    own_layer = pltpu.make_async_copy(layer, feats.at[group], local_sem.at[3])
    own_layer.start()

    for copy in tables:
        copy.wait()
    own_signal.wait()
    own_layer.wait()
    for copy in signals:
        copy.wait_recv()

    tile = 2 * rows

    def forward_step(index, carry):
        low = pl.ds(pl.multiple_of(index * tile, tile), tile)
        high = pl.ds(pl.multiple_of(span + index * tile, tile), tile)
        operand = jnp.concatenate([recv[0], recv[1], recv[2]], axis=1)
        real = jnp.dot(forward[low, :], operand, preferred_element_type=jnp.float32)
        other = jnp.dot(forward[high, :], operand, preferred_element_type=jnp.float32)
        m, h, g = [(real[:, i * share : (i + 1) * share], other[:, i * share : (i + 1) * share])
                   for i in range(3)]
        for i, pair in enumerate((product(*m, *h), against(*g, *h), against(*g, *m))):
            prods[low, i * share : (i + 1) * share] = pair[0].astype(jnp.bfloat16)
            prods[high, i * share : (i + 1) * share] = pair[1].astype(jnp.bfloat16)
        return carry

    lax.fori_loop(0, span // tile, forward_step, 0)

    for copy in gathers:
        copy.wait_recv()

    def feature_block(index):
        return feats.at[index * held // width, :,
                        pl.ds(pl.multiple_of(index * held % width, held), held)]

    sent_columns = []
    for d in range(1, blocks):
        peer = (me + d) % blocks
        copy = remote(feature_block(peer), columns.at[block_rows(me), :],
                      col_send, col_recv, d - 1, {"seq": peer})
        copy.start()
        sent_columns.append(copy)
    own_columns = pltpu.make_async_copy(
        feature_block(me), columns.at[block_rows(me), :], local_sem.at[4])
    own_columns.start()

    def inverse_step(index, carry):
        part = pl.ds(pl.multiple_of(index * tile, tile), tile)
        total = jnp.dot(inverse[part, :], prods[...], preferred_element_type=jnp.float32)
        total = total * (1.0 / span)
        res[0, part, :] = total[:, :share].astype(jnp.bfloat16)
        back = total[:, share : 2 * share].astype(jnp.bfloat16)
        res[1, part, :] = back
        res[2, part, :] = (total[:, 2 * share :] * scale_root).astype(jnp.bfloat16)
        own_value[part, :] = times(back, recv[3, part, :])
        return carry

    halves = [pl.ds(0, span // 2), pl.ds(span // 2, span // 2)]
    steps = span // tile // 2
    sent_values = []
    for half, part in enumerate(halves):
        lax.fori_loop(half * steps, half * steps + steps, inverse_step, 0)
        for d in range(1, chips + 1):
            peer = 2 * ((chip + d) % chips) + core if d < chips else sibling
            copy = remote(own_value.at[part, :], values.at[part, lanes(me)],
                          val_send, val_recv, half * chips + d - 1, {"seq": peer})
            copy.start()
            sent_values.append(copy)
    results = []
    for d in range(1, blocks):
        peer = (me + d) % blocks
        copy = remote(res.at[:, block_rows(peer), :], rest.at[:, :, lanes(me)],
                      res_send, res_recv, d - 1, {"seq": peer})
        copy.start()
        results.append(copy)
    own_result = pltpu.make_async_copy(
        res.at[:, block_rows(me), :], rest.at[:, :, lanes(me)], local_sem.at[5])
    own_result.start()
    own_column_value = pltpu.make_async_copy(own_value, values.at[:, lanes(me)], local_sem.at[6])
    own_column_value.start()

    own_columns.wait()
    for copy in sent_columns:
        copy.wait_recv()

    def turn_step(index, carry):
        part = pl.ds(pl.multiple_of(index * rows, rows), rows)
        columns_t[:, part] = columns[part, :].T
        return carry

    lax.fori_loop(0, blocks, turn_step, 0)

    wide = 2 * share

    def weigh(index):
        part = lanes(index, wide)
        out_weight[:, part] = scale_root * jnp.dot(
            columns_t[...], values[:, part], preferred_element_type=jnp.float32)

    passed_on = []
    for half, part in enumerate(halves):
        for d in range(1, chips):
            sent_values[half * chips + d - 1].wait_recv()
            block = values.at[part, lanes(2 * ((chip + chips - d) % chips) + core)]
            copy = remote(block, block, fwd_send, fwd_recv, half * chips + d - 1,
                          {"seq": sibling})
            copy.start()
            passed_on.append(copy)

    own_column_value.wait()
    for half in range(2):
        sent_values[half * chips + chips - 1].wait_recv()
    weigh(chip)
    for d in range(1, chips):
        for half in range(2):
            passed_on[half * (chips - 1) + d - 1].wait_recv()
        weigh((chip + chips - d) % chips)

    own_result.wait()
    for copy in results:
        copy.wait_recv()
    out_query[...] = times(cotangent[...], rest[0])
    out_key[...] = times(rest[1], value[...])
    out_value[...] = times(rest[1], key[...])
    out_filter[...] = rest[2]
    for copy in signals + gathers + sent_columns + sent_values + results + passed_on:
        copy.wait_send()


def fused(layer_input, gate_query, gate_key, value_proj, grad_out, filter_taps):
    rows, width = gate_query.shape
    blocks = lax.axis_size("seq")
    groups = lax.axis_size("chan")
    length = rows * blocks
    share = width // blocks
    held = width * groups // blocks
    table = half_shift_table(length)
    kind = gate_query.dtype
    vmem = pl.BlockSpec(memory_space=pltpu.VMEM)
    hbm = pl.BlockSpec(memory_space=pltpu.HBM)
    dma = pltpu.SemaphoreType.DMA
    signal = jax.ShapeDtypeStruct((rows, width), kind)
    return pl.pallas_call(
        functools.partial(fused_kernel, blocks, groups, 1.0 / math.sqrt(length)),
        out_shape=[signal] * 4 + [jax.ShapeDtypeStruct((held, width), jnp.float32)],
        in_specs=[hbm] * 8,
        out_specs=[vmem] * 5,
        scratch_shapes=[pltpu.VMEM((rows, width), kind)] * 6 + [
            pltpu.VMEM((4, rows, width), kind),
            pltpu.VMEM((4, length, share), kind),
            pltpu.VMEM((groups, rows, width), kind),
            pltpu.VMEM((length, held), kind),
            pltpu.VMEM((held, length), kind),
            pltpu.VMEM((2 * length, 3 * share), kind),
            pltpu.VMEM((length, share), kind),
            pltpu.VMEM((3, length, share), kind),
            pltpu.VMEM((3, rows, width), kind),
            pltpu.VMEM((length, width), kind),
            pltpu.VMEM((2 * length, length), kind),
            pltpu.VMEM((length, 2 * length), kind),
            dma((blocks - 1,)), dma((blocks - 1,)),
            dma((groups,)), dma((groups,)),
            dma((blocks - 1,)), dma((blocks - 1,)),
            dma((blocks - 1,)), dma((blocks - 1,)),
            dma((blocks,)), dma((blocks,)),
            dma((blocks,)), dma((blocks,)),
            dma((8,)), dma((6,)),
        ],
        compiler_params=pltpu.CompilerParams(
            collective_id=0, has_side_effects=True, vmem_limit_bytes=48 * 2**20
        ),
    )(*[pltpu.with_memory_space_constraint(x, pltpu.HBM) for x in (
        layer_input, gate_query, gate_key, value_proj, grad_out, filter_taps)],
      jnp.asarray(table), jnp.asarray(np.ascontiguousarray(table.T)))


def body(*arrays):
    rows, width = arrays[1].shape
    blocks = lax.axis_size("seq")
    share = width // blocks
    if share % 128 == 0 and rows % 16 == 0 and blocks % 2 == 0 and rows * blocks <= width:
        return tuple(fused(*arrays))
    return shards(*arrays)


def solution(mesh):
    spec = P("seq", "chan")
    return jax.shard_map(
        body, mesh=mesh, in_specs=(spec,) * 6, out_specs=(spec,) * 5, check_vma=False
    )
```
